32 devices in a mesh: runs: 2 (over y), tm: 16 (over z, x, core).
Axes of the slice: x: 2, y: 2, z: 4, core: 2. Of those that a mesh axis runs over, the one named last changes fastest.
Arguments:
- frames: float32 [32, 64, 2048], P(('runs', 'tm')), parts along dimension 0, may hold values from -12 to 12
- validity: int32 [32, 128], P(('runs', 'tm')), parts along dimension 0, may hold values 0 or 1
- anchors: int32 [4], P('runs'), parts along dimension 0, may hold values from 0 to 31
Outputs:
- planes: float32 [8, 32, 32, 128], P('runs', None, None, 'tm'), parts along dimension 0
The draws below stay inside these ranges and needn't reach their ends.
There are 2 independent parts, one for each index of `runs`. The reference program is written for one: setup_inputs(seed, part) draws one part's arguments, and reference() takes and returns one part's arrays. A program takes and returns all parts, laid end to end along the dimension named above; each array names one. Nothing has to cross between parts.
All inputs are finite; a program needn't handle non-finite values. No bound on the sum of `validity` on one device may be relied on, other than what follows from the above.
Results may differ from the reference program's by a relative error of at most 0.0003.
Values sent between devices are 32-bit elements; how exact they have to be, the bound alone decides.
A program may use at most 128 MiB of HBM per device.

```python
import jax
import jax.numpy as jnp
from jax import lax

WIN = 64
W = 2048
ROWS = 64
OFFSETS = 4
FRAMES = 16
STRIDE = 32
WR = 2
REGIONS = 128
CROP = 32


def draw_frames(key, part):
    pattern_key, speckle_key = jax.random.split(key, 2)
    pattern = jax.random.normal(pattern_key, (ROWS, W), jnp.float32)
    speckle = 0.5 * jax.random.normal(speckle_key, (FRAMES, ROWS, W), jnp.float32)

    def displaced(amount):
        return jnp.roll(jnp.roll(pattern, amount, axis=0), amount, axis=1)
    shifted = jax.vmap(displaced)(jnp.arange(FRAMES, dtype=jnp.int32))
    return jnp.clip(shifted + speckle, -12.0, 12.0)


def with_ends(entries, key, low, top_value):
    extent = entries.shape
    spot = [jax.random.randint(jax.random.fold_in(key, axis), (), 0, extent[axis]) for axis in range(len(extent))]
    entries = entries.at[tuple(spot)].set(low)
    longest = extent.index(max(extent))
    spot[longest] = (spot[longest] + 1) % extent[longest]
    return entries.at[tuple(spot)].set(top_value)


def setup_inputs(seed: int = 0, part: int = 0) -> dict:
    key_list = jax.random.split(jax.random.key(seed), 4)
    own_keys = jax.random.split(jax.random.fold_in(key_list[3], part), 4)
    return {
        "frames": draw_frames(jax.random.fold_in(jax.random.fold_in(key_list[3], part), 71), part),
        "validity": with_ends((jax.random.randint(own_keys[1], (FRAMES, REGIONS), 0, 4) < 3).astype(jnp.int32), jax.random.fold_in(own_keys[1], 1), 0, 1),
        "anchors": jax.random.randint(own_keys[2], (2,), 0, STRIDE).astype(jnp.int32),
    }


def cut_windows(padded, row_start, col_start, block_rows, window, columns):
    stride = window // 2
    across = columns // stride
    region = lax.dynamic_slice(padded, (row_start, col_start), (stride * (block_rows + 1), columns + stride))
    pieces = region.reshape(block_rows + 1, stride, across + 1, stride)
    stacked = jnp.concatenate([pieces[:-1], pieces[1:]], axis=1)
    joined = jnp.concatenate([stacked[:, :, :-1], stacked[:, :, 1:]], axis=3)
    windows = joined.transpose(1, 3, 0, 2).reshape(window, window, block_rows * across)
    return windows - jnp.mean(windows, axis=(0, 1), keepdims=True)


def reference(frames, validity, anchors):
    stride = WIN // 2
    distances = (1, 2, 4, 8)
    weights = validity.astype(jnp.float32)

    def spectra_of(frame_index):
        current = lax.dynamic_index_in_dim(frames, frame_index, 0, keepdims=False)
        padded = jnp.pad(current, ((0, 2 * stride), (0, 2 * stride)))
        windows = cut_windows(padded, anchors[0], anchors[1], WR, WIN, W)
        return jnp.fft.fft2(windows, axes=(0, 1))

    def step(totals, frame_index):
        own_spectrum = spectra_of(frame_index)
        own_weight = lax.dynamic_index_in_dim(weights, frame_index, 0, keepdims=False)
        real_parts = []
        imag_parts = []
        for distance in distances:
            later_index = frame_index + distance
            inside = (later_index < FRAMES).astype(jnp.float32)
            partner_index = jnp.minimum(later_index, FRAMES - 1)
            partner_spectrum = spectra_of(partner_index)
            partner_weight = lax.dynamic_index_in_dim(weights, partner_index, 0, keepdims=False)
            weight = own_weight * partner_weight * inside
            cross = jnp.conj(own_spectrum) * partner_spectrum
            real_parts.append(jnp.real(cross) * weight)
            imag_parts.append(jnp.imag(cross) * weight)
        return (totals[0] + jnp.stack(real_parts), totals[1] + jnp.stack(imag_parts)), None

    zeros = jnp.zeros((OFFSETS, WIN, WIN, REGIONS), jnp.float32)
    totals, _ = lax.scan(step, (zeros, zeros), jnp.arange(FRAMES))
    summed = lax.complex(totals[0], totals[1])
    full = jnp.real(jnp.fft.ifft2(summed, axes=(1, 2)))
    lag_index = (jnp.arange(CROP) - WIN // 4) % WIN
    cropped = full[:, lag_index][:, :, lag_index]
    scales = jnp.array([1.0 / ((FRAMES - distance) * WIN * WIN) for distance in distances], jnp.float32)
    return (cropped * scales[:, None, None, None]).astype(jnp.float32)
```

```python
import functools
import math

import jax
import jax.numpy as jnp
import ml_dtypes
import numpy as np
from jax import lax
from jax.experimental import pallas as pl
from jax.experimental.pallas import tpu as pltpu
from jax.sharding import PartitionSpec as P

WIN = 64


PRECISE = lax.Precision.HIGHEST
DISTANCES = (1, 2, 4, 8)


def shifted_2(block, axis, distance):
    devices = range(lax.axis_size(axis))
    route = [(i - distance, i) for i in devices if i - distance in devices]
    return lax.ppermute(block, axis, route)


def tables(window, lag_count):
    grid = jnp.arange(window, dtype=jnp.int32)
    phase = grid[:, None] * grid[None, :] % window
    angle = phase.astype(jnp.float32) * (2.0 * math.pi / window)
    cosine = jnp.cos(angle)
    minus_sine = -jnp.sin(angle)
    first_table = jnp.stack([cosine, minus_sine], axis=1)
    second_table = jnp.stack(
        [jnp.stack([cosine, -minus_sine], axis=-1), jnp.stack([minus_sine, cosine], axis=-1)],
        axis=1,
    )
    shifted = (jnp.arange(lag_count, dtype=jnp.int32) - window // 4) % window
    back_phase = shifted[:, None] * grid[None, :] % window
    back_angle = back_phase.astype(jnp.float32) * (2.0 * math.pi / window)
    back_cos = jnp.cos(back_angle)
    back_sin = jnp.sin(back_angle)
    third_table = jnp.stack(
        [jnp.stack([back_cos.T, back_sin.T], axis=1), jnp.stack([-back_sin.T, back_cos.T], axis=1)],
        axis=0,
    )
    fourth_table = jnp.stack([back_cos, -back_sin], axis=-1)
    return (first_table, second_table, third_table, fourth_table)


def cut_windows(padded, row_start, col_start, block_rows, window, columns):
    stride = window // 2
    across = columns // stride
    region = lax.dynamic_slice(
        padded, (row_start, col_start), (stride * (block_rows + 1), columns + stride)
    )
    pieces = region.reshape(block_rows + 1, stride, across + 1, stride)
    stacked = jnp.concatenate([pieces[:-1], pieces[1:]], axis=1)
    joined = jnp.concatenate([stacked[:, :, :-1], stacked[:, :, 1:]], axis=3)
    windows = joined.transpose(1, 3, 0, 2).reshape(window, window, block_rows * across)
    return windows - jnp.mean(windows, axis=(0, 1), keepdims=True)


def spectrum(windows, first_table, second_table):
    half = jnp.einsum("ijr,jck->ickr", windows, first_table, precision=PRECISE)
    return jnp.einsum("pdic,ickr->pdkr", second_table, half, precision=PRECISE)


def cross_of(own_spectrum, later_spectrum, weight):
    own_real = own_spectrum[:, 0]
    own_imag = own_spectrum[:, 1]
    late_real = later_spectrum[:, 0]
    late_imag = later_spectrum[:, 1]
    cross_real = (own_real * late_real + own_imag * late_imag) * weight
    cross_imag = (own_real * late_imag - own_imag * late_real) * weight
    return jnp.stack([cross_real, cross_imag], axis=1)


def back_transform(cross, third_table, fourth_table):
    middle = jnp.einsum("pckr,ckdv->pdvr", cross, third_table, precision=PRECISE)
    return jnp.einsum("pdvr,upd->uvr", middle, fourth_table, precision=PRECISE)


def body(frames, validity, anchors):
    current = frames[0]
    pixel_rows, columns = current.shape
    window = WIN
    stride = window // 2
    window_rows = pixel_rows // stride
    lag_count = window // 2
    total_frames = lax.axis_size("tm")
    position = lax.axis_index("tm")
    first_table, second_table, third_table, fourth_table = tables(window, lag_count)
    own_valid = validity[0].astype(jnp.float32)
    padded_own = jnp.pad(current, ((0, 2 * stride), (0, 2 * stride)))
    windows = cut_windows(padded_own, anchors[0], anchors[1], window_rows, window, columns)
    own_spectrum = spectrum(windows, first_table, second_table)
    results = []
    for distance in DISTANCES:
        partner, partner_valid = shifted_2((own_spectrum, own_valid), "tm", -distance)
        later_index = position + distance
        inside = (later_index < total_frames).astype(jnp.float32)
        scale = 1.0 / (float(total_frames - distance) * float(window) ** 4)
        weight = own_valid * partner_valid * inside * scale
        results.append(
            back_transform(cross_of(own_spectrum, partner, weight), third_table, fourth_table)
        )
    partial_value = jnp.stack(results)
    return lax.psum_scatter(partial_value, "tm", scatter_dimension=3, tiled=True)


GROUP = 16
BF = jnp.bfloat16
F32 = jnp.float32


def halves(table):
    table = table.astype(np.float32)
    high = table.astype(ml_dtypes.bfloat16)
    low = (table - high.astype(np.float32)).astype(ml_dtypes.bfloat16)
    return high, low


@functools.cache
def constant_tables():
    unit = 2.0 * np.pi / 64
    cols = np.arange(160)[:, None]
    wide = np.zeros((160, 384))
    k = np.arange(32)[None, :]
    for b in range(4):
        inside = (cols >= 32 * b) & (cols < 32 * b + 64)
        wide[:, 32 * b : 32 * b + 32] = np.cos(unit * (cols * k % 64)) * inside
        wide[:, 128 + 32 * b : 160 + 32 * b] = -np.sin(unit * (cols * k % 64)) * inside
        wide[:, 256 + b] = ((1 - 2 * (cols % 2)) * inside)[:, 0]
    high, low = halves(wide)
    w1 = np.concatenate([high[:128], high[:128]], axis=0)
    w2 = np.concatenate(
        [low[:128], high[128:], high[128:], low[128:], np.zeros_like(low[128:])], axis=0
    )
    p = np.arange(64)
    angle = unit * (p[:, None] * p[None, :] % 64)
    high, low = halves(np.concatenate([np.cos(angle), np.sin(angle)] * 2, axis=0))
    m = np.concatenate([high, high, low], axis=1)
    u = np.arange(32) - 16
    angle = unit * (u[:, None] * p[None, :] % 64)
    cosine, sine = np.cos(angle), np.sin(angle)
    high, low = halves(
        np.concatenate(
            [np.concatenate([cosine, -sine], axis=1), np.concatenate([sine, cosine], axis=1)],
            axis=0,
        )
    )
    g = np.concatenate([high, high, low], axis=1)
    back = np.zeros((384, 128))
    twice = np.where(np.arange(32) == 0, 1.0, 2.0)[:, None]
    angle = unit * (np.arange(32)[:, None] * u[None, :] % 64)
    for b in range(4):
        span = slice(32 * b, 32 * b + 32)
        back[span, span] = twice * np.cos(angle)
        back[128 + b, span] = 1 - 2 * (u % 2)
        back[256 + 32 * b : 288 + 32 * b, span] = -twice * np.sin(angle)
    high, low = halves(back)
    h = np.concatenate([high, low], axis=1)
    return w1, w2, m, g, h


def column_block(device):
    return lax.rem(device, 8) * 2 + device // 8


def split(value):
    high = value.astype(BF)
    return high, (value - high.astype(F32)).astype(BF)


def dot(left, right):
    return jnp.dot(left, right, preferred_element_type=F32)


def kernel(
    anchor_ref, x_ref, v_ref, w1_ref, w2_ref, m_ref, g_ref, h_ref, out_ref,
    pack, recv, mask_m, expand, sre, sim, cross, lag, plane,
    send_sem, recv_sem, plane_send, plane_recv,
):
    me = lax.axis_index("tm")
    side = me // 8
    partner = lax.rem(me + 8, GROUP)
    mine = column_block(me)

    barrier = pltpu.get_barrier_semaphore()
    for step in range(1, GROUP):
        peer = lax.rem(me + step, GROUP)
        pl.semaphore_signal(
            barrier, inc=1, device_id={"tm": peer}, device_id_type=pl.DeviceIdType.MESH
        )

    row_start = anchor_ref[0]
    col_start = anchor_ref[1]

    lane = lax.broadcasted_iota(jnp.int32, (64, 128), 1)
    lane16 = lax.broadcasted_iota(jnp.int32, (16, 128), 1)
    keep = lane < 128 - col_start
    amount = lax.rem(128 - col_start, 128)
    valid_row = jnp.broadcast_to(v_ref[...].astype(F32), (8, 128))
    following = jnp.zeros((64, 128), F32)
    halo = jnp.zeros((16, 128), F32)
    for block in reversed(range(GROUP)):
        rolled = pltpu.roll(x_ref[:, 128 * block : 128 * block + 128], amount, 1)
        shifted = jnp.where(keep, rolled, following)
        pack[block, 0:64, :] = shifted
        pack[block, 64:80, :] = halo
        pack[block, 80:88, :] = valid_row
        following = rolled
        halo = shifted[0:16]
        for group in range(1, 4):
            moved = pltpu.roll(shifted[16 * group : 16 * group + 16], 32 * group, 1)
            halo = jnp.where(lane16 >= 32 * group, moved, halo)

    pl.semaphore_wait(barrier, GROUP - 1)

    def transfer(source, target):
        return pltpu.make_async_remote_copy(
            src_ref=pack.at[column_block(target)],
            dst_ref=recv.at[source],
            send_sem=send_sem.at[target],
            recv_sem=recv_sem.at[source],
            device_id={"tm": target},
            device_id_type=pl.DeviceIdType.MESH,
        )

    for step in range(1, GROUP):
        transfer(me, lax.rem(me + step, GROUP)).start()

    row = lax.rem(lax.broadcasted_iota(jnp.int32, (256, 192), 1), 64)
    below = row_start + 32 * (lax.broadcasted_iota(jnp.int32, (256, 192), 0) // 128)
    mask_m[...] = jnp.where(row >= below, m_ref[...].astype(F32), 0.0).astype(BF)
    region = lax.broadcasted_iota(jnp.int32, (128, 512), 0)
    place = lax.broadcasted_iota(jnp.int32, (128, 512), 1)
    inner = lax.rem(place, 256)
    which = jnp.where(inner < 128, inner // 32, inner - 128)
    wanted = 64 * (place // 256) + 4 * mine + which
    expand[...] = jnp.where((region == wanted) & (which < 4), 1.0, 0.0).astype(BF)

    def spectra(t):
        main_high, main_low = split(recv[t, 0:64, :])
        edge = recv[t, 64:80, :]
        edge_high = edge.astype(BF).astype(F32)
        edge_low = edge - edge_high
        tiles = []
        for group in range(4):
            first = pltpu.roll(edge_high, (128 - 32 * group) % 128, 1)
            second = pltpu.roll(edge_low, (160 - 32 * group) % 128, 1)
            third = pltpu.roll(edge_high, (192 - 32 * group) % 128, 1)
            tile = jnp.where(lane16 < 32, first, jnp.where(lane16 < 64, second, third))
            tiles.append(jnp.where(lane16 < 96, tile, 0.0))
        edges = jnp.concatenate(tiles, axis=0).astype(BF)
        half = dot(jnp.concatenate([main_high, main_low], axis=1), w1_ref[...])
        half += dot(jnp.concatenate([main_high, edges], axis=1), w2_ref[...])
        half_high, half_low = split(half)
        full = dot(mask_m[...], jnp.concatenate([half_high, half_low, half_high], axis=0))
        usable = dot(recv[t, 80:88, :].astype(BF), expand[...])[0:1, :]
        for a in range(2):
            cos_part = full[128 * a : 128 * a + 64]
            sin_part = full[128 * a + 64 : 128 * a + 128]
            weight = usable[:, 256 * a : 256 * a + 256]
            sre[t, a, :, 0:128] = (cos_part[:, 0:128] + sin_part[:, 128:256]) * weight[:, 0:128]
            sim[t, a, :, 0:128] = (cos_part[:, 128:256] - sin_part[:, 0:128]) * weight[:, 0:128]
            sre[t, a, :, 128:256] = cos_part[:, 256:384] * weight[:, 128:256]
            sim[t, a, :, 128:256] = -sin_part[:, 256:384] * weight[:, 128:256]

    recv[me] = pack[mine]
    spectra(me)

    def arrive(step, carry):
        source = lax.rem(me - step + GROUP, GROUP)
        transfer(source, me).wait_recv()
        spectra(source)
        return carry

    lax.fori_loop(1, GROUP, arrive, 0)

    def correlate(index, carry):
        a = index // 8
        start = pl.multiple_of(lax.rem(index, 8) * 8, 8)
        line = lax.broadcasted_iota(jnp.int32, (8, 128), 0) + start
        column = lax.rem(lax.broadcasted_iota(jnp.int32, (8, 128), 1), 32)
        for part in range(2):
            lanes = slice(128 * part, 128 * part + 128)
            real = [sre[t, a, pl.ds(start, 8), lanes] for t in range(GROUP)]
            imag = [sim[t, a, pl.ds(start, 8), lanes] for t in range(GROUP)]
            for e, distance in enumerate(DISTANCES):
                total_real = jnp.zeros((8, 128), F32)
                total_imag = jnp.zeros((8, 128), F32)
                for t in range(GROUP - distance):
                    later = t + distance
                    total_real += real[t] * real[later] + imag[t] * imag[later]
                    total_imag += real[t] * imag[later] - imag[t] * real[later]
                scale = 1.0 / (float(GROUP - distance) * float(WIN) ** 4)
                if part == 0:
                    alive = (line > 0) | (column > 0)
                    total_real = jnp.where(alive, total_real, 0.0)
                    total_imag = jnp.where(alive, total_imag, 0.0)
                cross[e, a, pl.ds(start, 8), lanes] = total_real * scale
                cross[e, a, pl.ds(start + 64, 8), lanes] = total_imag * scale
        return carry

    lax.fori_loop(0, 16, correlate, 0)

    def back(a):
        for e in range(4):
            high, low = split(cross[e, a])
            middle = dot(g_ref[...], jnp.concatenate([high, low, high], axis=0))
            lag[32 * e : 32 * e + 32, 0:256] = middle[0:32]
            lag[32 * e : 32 * e + 32, 256:384] = middle[32:64, 0:128]
        high, low = split(lag[...])
        both = dot(high, h_ref[...])
        return both[:, 0:128] + both[:, 128:256] + dot(low, h_ref[:, 0:128])

    plane[...] = back(1 - side)
    give = pltpu.make_async_remote_copy(
        src_ref=plane,
        dst_ref=out_ref.at[side],
        send_sem=plane_send,
        recv_sem=plane_recv,
        device_id={"tm": partner},
        device_id_type=pl.DeviceIdType.MESH,
    )
    give.start()
    out_ref[side] = back(side)
    for step in range(1, GROUP):
        transfer(me, lax.rem(me + step, GROUP)).wait_send()
    give.wait_send()
    pltpu.make_async_remote_copy(
        src_ref=plane,
        dst_ref=out_ref.at[1 - side],
        send_sem=plane_send,
        recv_sem=plane_recv,
        device_id={"tm": partner},
        device_id_type=pl.DeviceIdType.MESH,
    ).wait_recv()


def group_body(frames, validity, anchors):
    tables_in = [jnp.asarray(table) for table in constant_tables()]
    vmem = pl.BlockSpec(memory_space=pltpu.VMEM)
    halves_out = pl.pallas_call(
        kernel,
        out_shape=jax.ShapeDtypeStruct((2, 128, 128), F32),
        in_specs=[pl.BlockSpec(memory_space=pltpu.SMEM)] + [vmem] * 7,
        out_specs=vmem,
        scratch_shapes=[
            pltpu.VMEM((GROUP, 88, 128), F32),
            pltpu.VMEM((GROUP, 88, 128), F32),
            pltpu.VMEM((256, 192), BF),
            pltpu.VMEM((128, 512), BF),
            pltpu.VMEM((GROUP, 2, 64, 256), F32),
            pltpu.VMEM((GROUP, 2, 64, 256), F32),
            pltpu.VMEM((4, 2, 128, 256), F32),
            pltpu.VMEM((128, 384), F32),
            pltpu.VMEM((128, 128), F32),
            pltpu.SemaphoreType.DMA((GROUP,)),
            pltpu.SemaphoreType.DMA((GROUP,)),
            pltpu.SemaphoreType.DMA,
            pltpu.SemaphoreType.DMA,
        ],
        compiler_params=pltpu.CompilerParams(
            collective_id=0, has_side_effects=True, vmem_limit_bytes=40 * 1024 * 1024
        ),
    )(anchors, frames[0], validity, *tables_in)
    parts = halves_out.reshape(2, 4, 32, 4, 32)
    return parts.transpose(1, 2, 4, 0, 3).reshape(4, 32, 32, 8)


def solution(mesh):
    placed = (P(("runs", "tm"), None, None), P(("runs", "tm"), None), P("runs"))
    chosen = group_body if mesh.shape["tm"] == GROUP else body
    return jax.shard_map(
        chosen, mesh=mesh, in_specs=placed, out_specs=P("runs", None, None, "tm"), check_vma=False
    )
```

```python
import functools
import math

import jax
import jax.numpy as jnp
import ml_dtypes
import numpy as np
from jax import lax
from jax.experimental import pallas as pl
from jax.experimental.pallas import tpu as pltpu
from jax.sharding import PartitionSpec as P

WIN = 64


PRECISE = lax.Precision.HIGHEST
DISTANCES = (1, 2, 4, 8)


def shifted_2(block, axis, distance):
    devices = range(lax.axis_size(axis))
    route = [(i - distance, i) for i in devices if i - distance in devices]
    return lax.ppermute(block, axis, route)


def tables(window, lag_count):
    grid = jnp.arange(window, dtype=jnp.int32)
    phase = grid[:, None] * grid[None, :] % window
    angle = phase.astype(jnp.float32) * (2.0 * math.pi / window)
    cosine = jnp.cos(angle)
    minus_sine = -jnp.sin(angle)
    first_table = jnp.stack([cosine, minus_sine], axis=1)
    second_table = jnp.stack(
        [jnp.stack([cosine, -minus_sine], axis=-1), jnp.stack([minus_sine, cosine], axis=-1)],
        axis=1,
    )
    shifted = (jnp.arange(lag_count, dtype=jnp.int32) - window // 4) % window
    back_phase = shifted[:, None] * grid[None, :] % window
    back_angle = back_phase.astype(jnp.float32) * (2.0 * math.pi / window)
    back_cos = jnp.cos(back_angle)
    back_sin = jnp.sin(back_angle)
    third_table = jnp.stack(
        [jnp.stack([back_cos.T, back_sin.T], axis=1), jnp.stack([-back_sin.T, back_cos.T], axis=1)],
        axis=0,
    )
    fourth_table = jnp.stack([back_cos, -back_sin], axis=-1)
    return (first_table, second_table, third_table, fourth_table)


def cut_windows(padded, row_start, col_start, block_rows, window, columns):
    stride = window // 2
    across = columns // stride
    region = lax.dynamic_slice(
        padded, (row_start, col_start), (stride * (block_rows + 1), columns + stride)
    )
    pieces = region.reshape(block_rows + 1, stride, across + 1, stride)
    stacked = jnp.concatenate([pieces[:-1], pieces[1:]], axis=1)
    joined = jnp.concatenate([stacked[:, :, :-1], stacked[:, :, 1:]], axis=3)
    windows = joined.transpose(1, 3, 0, 2).reshape(window, window, block_rows * across)
    return windows - jnp.mean(windows, axis=(0, 1), keepdims=True)


def spectrum(windows, first_table, second_table):
    half = jnp.einsum("ijr,jck->ickr", windows, first_table, precision=PRECISE)
    return jnp.einsum("pdic,ickr->pdkr", second_table, half, precision=PRECISE)


def cross_of(own_spectrum, later_spectrum, weight):
    own_real = own_spectrum[:, 0]
    own_imag = own_spectrum[:, 1]
    late_real = later_spectrum[:, 0]
    late_imag = later_spectrum[:, 1]
    cross_real = (own_real * late_real + own_imag * late_imag) * weight
    cross_imag = (own_real * late_imag - own_imag * late_real) * weight
    return jnp.stack([cross_real, cross_imag], axis=1)


def back_transform(cross, third_table, fourth_table):
    middle = jnp.einsum("pckr,ckdv->pdvr", cross, third_table, precision=PRECISE)
    return jnp.einsum("pdvr,upd->uvr", middle, fourth_table, precision=PRECISE)


def body(frames, validity, anchors):
    current = frames[0]
    pixel_rows, columns = current.shape
    window = WIN
    stride = window // 2
    window_rows = pixel_rows // stride
    lag_count = window // 2
    total_frames = lax.axis_size("tm")
    position = lax.axis_index("tm")
    first_table, second_table, third_table, fourth_table = tables(window, lag_count)
    own_valid = validity[0].astype(jnp.float32)
    padded_own = jnp.pad(current, ((0, 2 * stride), (0, 2 * stride)))
    windows = cut_windows(padded_own, anchors[0], anchors[1], window_rows, window, columns)
    own_spectrum = spectrum(windows, first_table, second_table)
    results = []
    for distance in DISTANCES:
        partner, partner_valid = shifted_2((own_spectrum, own_valid), "tm", -distance)
        later_index = position + distance
        inside = (later_index < total_frames).astype(jnp.float32)
        scale = 1.0 / (float(total_frames - distance) * float(window) ** 4)
        weight = own_valid * partner_valid * inside * scale
        results.append(
            back_transform(cross_of(own_spectrum, partner, weight), third_table, fourth_table)
        )
    partial_value = jnp.stack(results)
    return lax.psum_scatter(partial_value, "tm", scatter_dimension=3, tiled=True)


GROUP = 16
BF = jnp.bfloat16
F32 = jnp.float32


def halves(table):
    table = table.astype(np.float32)
    high = table.astype(ml_dtypes.bfloat16)
    low = (table - high.astype(np.float32)).astype(ml_dtypes.bfloat16)
    return high, low


@functools.cache
def constant_tables():
    unit = 2.0 * np.pi / 64
    cols = np.arange(160)[:, None]
    wide = np.zeros((160, 384))
    k = np.arange(32)[None, :]
    for b in range(4):
        inside = (cols >= 32 * b) & (cols < 32 * b + 64)
        wide[:, 32 * b : 32 * b + 32] = np.cos(unit * (cols * k % 64)) * inside
        wide[:, 128 + 32 * b : 160 + 32 * b] = -np.sin(unit * (cols * k % 64)) * inside
        wide[:, 256 + b] = ((1 - 2 * (cols % 2)) * inside)[:, 0]
    high, low = halves(wide)
    w1 = np.concatenate([high[:128], high[:128]], axis=0)
    w2 = np.concatenate(
        [low[:128], high[128:], high[128:], low[128:], np.zeros_like(low[128:])], axis=0
    )
    p = np.arange(64)
    angle = unit * (p[:, None] * p[None, :] % 64)
    high, low = halves(np.concatenate([np.cos(angle), np.sin(angle)] * 2, axis=0))
    m = np.concatenate([high, high, low], axis=1)
    u = np.arange(32) - 16
    angle = unit * (u[:, None] * p[None, :] % 64)
    cosine, sine = np.cos(angle), np.sin(angle)
    high, low = halves(
        np.concatenate(
            [np.concatenate([cosine, -sine], axis=1), np.concatenate([sine, cosine], axis=1)],
            axis=0,
        )
    )
    g = np.concatenate([high, high, low], axis=1)
    back = np.zeros((384, 128))
    twice = np.where(np.arange(32) == 0, 1.0, 2.0)[:, None]
    angle = unit * (np.arange(32)[:, None] * u[None, :] % 64)
    for b in range(4):
        span = slice(32 * b, 32 * b + 32)
        back[span, span] = twice * np.cos(angle)
        back[128 + b, span] = 1 - 2 * (u % 2)
        back[256 + 32 * b : 288 + 32 * b, span] = -twice * np.sin(angle)
    high, low = halves(back)
    h = np.concatenate([high, low], axis=1)
    return w1, w2, m, g, h


def column_block(device):
    return lax.rem(device, 8) * 2 + device // 8


def split(value):
    high = value.astype(BF)
    return high, (value - high.astype(F32)).astype(BF)


def dot(left, right):
    return jnp.dot(left, right, preferred_element_type=F32)


def kernel(
    anchor_hbm, x_hbm, v_hbm, w1_hbm, w2_hbm, m_hbm, g_hbm, h_hbm, out_ref,
    anchor_ref, x_ref, v_ref, w1_ref, w2_ref, m_ref, g_ref, h_ref, load_sem, pack, recv, mask_m, expand, sre, sim, cross, lag, plane,
    send_sem, recv_sem, plane_send, plane_recv,
):
    me = lax.axis_index("tm")
    side = me // 8
    partner = lax.rem(me + 8, GROUP)
    mine = column_block(me)

    barrier = pltpu.get_barrier_semaphore()
    for step in range(1, GROUP):
        peer = lax.rem(me + step, GROUP)
        pl.semaphore_signal(
            barrier, inc=1, device_id={"tm": peer}, device_id_type=pl.DeviceIdType.MESH
        )

    loads = [
        pltpu.make_async_copy(source, target, load_sem.at[index])
        for index, (source, target) in enumerate(
            [
                (anchor_hbm, anchor_ref),
                (x_hbm, x_ref),
                (v_hbm, v_ref),
                (m_hbm, m_ref),
                (w1_hbm, w1_ref),
                (w2_hbm, w2_ref),
                (g_hbm, g_ref),
                (h_hbm, h_ref),
            ]
        )
    ]
    for load in loads:
        load.start()
    for load in loads[:3]:
        load.wait()
    row_start = anchor_ref[0]
    col_start = anchor_ref[1]

    lane = lax.broadcasted_iota(jnp.int32, (64, 128), 1)
    lane16 = lax.broadcasted_iota(jnp.int32, (16, 128), 1)
    keep = lane < 128 - col_start
    amount = lax.rem(128 - col_start, 128)
    valid_row = jnp.broadcast_to(v_ref[...].astype(F32), (8, 128))
    following = jnp.zeros((64, 128), F32)
    halo = jnp.zeros((16, 128), F32)
    for block in reversed(range(GROUP)):
        rolled = pltpu.roll(x_ref[:, 128 * block : 128 * block + 128], amount, 1)
        shifted = jnp.where(keep, rolled, following)
        pack[block, 0:64, :] = shifted
        pack[block, 64:80, :] = halo
        pack[block, 80:88, :] = valid_row
        following = rolled
        halo = shifted[0:16]
        for group in range(1, 4):
            moved = pltpu.roll(shifted[16 * group : 16 * group + 16], 32 * group, 1)
            halo = jnp.where(lane16 >= 32 * group, moved, halo)

    pl.semaphore_wait(barrier, GROUP - 1)

    def transfer(source, target):
        return pltpu.make_async_remote_copy(
            src_ref=pack.at[column_block(target), pl.ds(0, 81)],
            dst_ref=recv.at[source, pl.ds(0, 81)],
            send_sem=send_sem.at[target],
            recv_sem=recv_sem.at[source],
            device_id={"tm": target},
            device_id_type=pl.DeviceIdType.MESH,
        )

    for step in range(8):
        transfer(me, 8 * (1 - side) + lax.rem(me + step, 8)).start()
    for step in range(1, 8):
        transfer(me, 8 * side + lax.rem(me + step, 8)).start()

    for load in loads[3:]:
        load.wait()
    row = lax.rem(lax.broadcasted_iota(jnp.int32, (256, 192), 1), 64)
    below = row_start + 32 * (lax.broadcasted_iota(jnp.int32, (256, 192), 0) // 128)
    mask_m[...] = jnp.where(row >= below, m_ref[...].astype(F32), 0.0).astype(BF)
    region = lax.broadcasted_iota(jnp.int32, (128, 512), 0)
    place = lax.broadcasted_iota(jnp.int32, (128, 512), 1)
    inner = lax.rem(place, 256)
    which = jnp.where(inner < 128, inner // 32, inner - 128)
    wanted = 64 * (place // 256) + 4 * mine + which
    expand[...] = jnp.where((region == wanted) & (which < 4), 1.0, 0.0).astype(BF)

    def spectra(t):
        main_high, main_low = split(recv[t, 0:64, :])
        edge = recv[t, 64:80, :]
        edge_high = edge.astype(BF).astype(F32)
        edge_low = edge - edge_high
        tiles = []
        for group in range(4):
            first = pltpu.roll(edge_high, (128 - 32 * group) % 128, 1)
            second = pltpu.roll(edge_low, (160 - 32 * group) % 128, 1)
            third = pltpu.roll(edge_high, (192 - 32 * group) % 128, 1)
            tile = jnp.where(lane16 < 32, first, jnp.where(lane16 < 64, second, third))
            tiles.append(jnp.where(lane16 < 96, tile, 0.0))
        edges = jnp.concatenate(tiles, axis=0).astype(BF)
        half = dot(jnp.concatenate([main_high, main_low], axis=1), w1_ref[...])
        half += dot(jnp.concatenate([main_high, edges], axis=1), w2_ref[...])
        half_high, half_low = split(half)
        full = dot(mask_m[...], jnp.concatenate([half_high, half_low, half_high], axis=0))
        usable = dot(jnp.broadcast_to(recv[t, 80:81, :], (8, 128)).astype(BF), expand[...])[0:1, :]
        for a in range(2):
            cos_part = full[128 * a : 128 * a + 64]
            sin_part = full[128 * a + 64 : 128 * a + 128]
            weight = usable[:, 256 * a : 256 * a + 256]
            sre[t, a, :, 0:128] = (cos_part[:, 0:128] + sin_part[:, 128:256]) * weight[:, 0:128]
            sim[t, a, :, 0:128] = (cos_part[:, 128:256] - sin_part[:, 0:128]) * weight[:, 0:128]
            sre[t, a, :, 128:256] = cos_part[:, 256:384] * weight[:, 128:256]
            sim[t, a, :, 128:256] = -sin_part[:, 256:384] * weight[:, 128:256]

    recv[me] = pack[mine]
    spectra(me)

    def arrive(step, carry):
        near = step < 8
        source = 8 * jnp.where(near, side, 1 - side) + lax.rem(me - step + GROUP, 8)
        transfer(source, me).wait_recv()
        spectra(source)
        return carry

    lax.fori_loop(1, GROUP, arrive, 0)

    def correlate(index, carry):
        a = index // 8
        start = pl.multiple_of(lax.rem(index, 8) * 8, 8)
        line = lax.broadcasted_iota(jnp.int32, (8, 128), 0) + start
        column = lax.rem(lax.broadcasted_iota(jnp.int32, (8, 128), 1), 32)
        for part in range(2):
            lanes = slice(128 * part, 128 * part + 128)
            real = [sre[t, a, pl.ds(start, 8), lanes] for t in range(GROUP)]
            imag = [sim[t, a, pl.ds(start, 8), lanes] for t in range(GROUP)]
            for e, distance in enumerate(DISTANCES):
                total_real = jnp.zeros((8, 128), F32)
                total_imag = jnp.zeros((8, 128), F32)
                for t in range(GROUP - distance):
                    later = t + distance
                    total_real += real[t] * real[later] + imag[t] * imag[later]
                    total_imag += real[t] * imag[later] - imag[t] * real[later]
                scale = 1.0 / (float(GROUP - distance) * float(WIN) ** 4)
                if part == 0:
                    alive = (line > 0) | (column > 0)
                    total_real = jnp.where(alive, total_real, 0.0)
                    total_imag = jnp.where(alive, total_imag, 0.0)
                cross[e, a, pl.ds(start, 8), lanes] = total_real * scale
                cross[e, a, pl.ds(start + 64, 8), lanes] = total_imag * scale
        return carry

    lax.fori_loop(0, 16, correlate, 0)

    def back(a):
        for e in range(4):
            high, low = split(cross[e, a])
            middle = dot(g_ref[...], jnp.concatenate([high, low, high], axis=0))
            lag[32 * e : 32 * e + 32, 0:256] = middle[0:32]
            lag[32 * e : 32 * e + 32, 256:384] = middle[32:64, 0:128]
        high, low = split(lag[...])
        both = dot(high, h_ref[...])
        return both[:, 0:128] + both[:, 128:256] + dot(low, h_ref[:, 0:128])

    plane[...] = back(1 - side)
    give = pltpu.make_async_remote_copy(
        src_ref=plane,
        dst_ref=out_ref.at[side],
        send_sem=plane_send,
        recv_sem=plane_recv,
        device_id={"tm": partner},
        device_id_type=pl.DeviceIdType.MESH,
    )
    give.start()
    out_ref[side] = back(side)
    for step in range(1, GROUP):
        transfer(me, lax.rem(me + step, GROUP)).wait_send()
    give.wait_send()
    pltpu.make_async_remote_copy(
        src_ref=plane,
        dst_ref=out_ref.at[1 - side],
        send_sem=plane_send,
        recv_sem=plane_recv,
        device_id={"tm": partner},
        device_id_type=pl.DeviceIdType.MESH,
    ).wait_recv()


def group_body(frames, validity, anchors):
    tables_in = [jnp.asarray(table) for table in constant_tables()]
    vmem = pl.BlockSpec(memory_space=pltpu.VMEM)
    halves_out = pl.pallas_call(
        kernel,
        out_shape=jax.ShapeDtypeStruct((2, 128, 128), F32),
        in_specs=[pl.BlockSpec(memory_space=pltpu.HBM)] * 8,
        out_specs=vmem,
        scratch_shapes=[
            pltpu.SMEM((2,), jnp.int32),
            pltpu.VMEM(frames.shape[1:], F32),
            pltpu.VMEM(validity.shape, jnp.int32),
            *[pltpu.VMEM(table.shape, BF) for table in tables_in],
            pltpu.SemaphoreType.DMA((8,)),
            pltpu.VMEM((GROUP, 88, 128), F32),
            pltpu.VMEM((GROUP, 88, 128), F32),
            pltpu.VMEM((256, 192), BF),
            pltpu.VMEM((128, 512), BF),
            pltpu.VMEM((GROUP, 2, 64, 256), F32),
            pltpu.VMEM((GROUP, 2, 64, 256), F32),
            pltpu.VMEM((4, 2, 128, 256), F32),
            pltpu.VMEM((128, 384), F32),
            pltpu.VMEM((128, 128), F32),
            pltpu.SemaphoreType.DMA((GROUP,)),
            pltpu.SemaphoreType.DMA((GROUP,)),
            pltpu.SemaphoreType.DMA,
            pltpu.SemaphoreType.DMA,
        ],
        compiler_params=pltpu.CompilerParams(
            collective_id=0, has_side_effects=True, vmem_limit_bytes=60 * 1024 * 1024
        ),
    )(anchors, frames[0], validity, *tables_in)
    parts = halves_out.reshape(2, 4, 32, 4, 32)
    return parts.transpose(1, 2, 4, 0, 3).reshape(4, 32, 32, 8)


def solution(mesh):
    placed = (P(("runs", "tm"), None, None), P(("runs", "tm"), None), P("runs"))
    chosen = group_body if mesh.shape["tm"] == GROUP else body
    return jax.shard_map(
        chosen, mesh=mesh, in_specs=placed, out_specs=P("runs", None, None, "tm"), check_vma=False
    )
```

```python
import functools
import math

import jax
import jax.numpy as jnp
import ml_dtypes
import numpy as np
from jax import lax
from jax.experimental import pallas as pl
from jax.experimental.pallas import tpu as pltpu
from jax.sharding import PartitionSpec as P

WIN = 64


PRECISE = lax.Precision.HIGHEST
DISTANCES = (1, 2, 4, 8)


def shifted_2(block, axis, distance):
    devices = range(lax.axis_size(axis))
    route = [(i - distance, i) for i in devices if i - distance in devices]
    return lax.ppermute(block, axis, route)


def tables(window, lag_count):
    grid = jnp.arange(window, dtype=jnp.int32)
    phase = grid[:, None] * grid[None, :] % window
    angle = phase.astype(jnp.float32) * (2.0 * math.pi / window)
    cosine = jnp.cos(angle)
    minus_sine = -jnp.sin(angle)
    first_table = jnp.stack([cosine, minus_sine], axis=1)
    second_table = jnp.stack(
        [jnp.stack([cosine, -minus_sine], axis=-1), jnp.stack([minus_sine, cosine], axis=-1)],
        axis=1,
    )
    shifted = (jnp.arange(lag_count, dtype=jnp.int32) - window // 4) % window
    back_phase = shifted[:, None] * grid[None, :] % window
    back_angle = back_phase.astype(jnp.float32) * (2.0 * math.pi / window)
    back_cos = jnp.cos(back_angle)
    back_sin = jnp.sin(back_angle)
    third_table = jnp.stack(
        [jnp.stack([back_cos.T, back_sin.T], axis=1), jnp.stack([-back_sin.T, back_cos.T], axis=1)],
        axis=0,
    )
    fourth_table = jnp.stack([back_cos, -back_sin], axis=-1)
    return (first_table, second_table, third_table, fourth_table)


def cut_windows(padded, row_start, col_start, block_rows, window, columns):
    stride = window // 2
    across = columns // stride
    region = lax.dynamic_slice(
        padded, (row_start, col_start), (stride * (block_rows + 1), columns + stride)
    )
    pieces = region.reshape(block_rows + 1, stride, across + 1, stride)
    stacked = jnp.concatenate([pieces[:-1], pieces[1:]], axis=1)
    joined = jnp.concatenate([stacked[:, :, :-1], stacked[:, :, 1:]], axis=3)
    windows = joined.transpose(1, 3, 0, 2).reshape(window, window, block_rows * across)
    return windows - jnp.mean(windows, axis=(0, 1), keepdims=True)


def spectrum(windows, first_table, second_table):
    half = jnp.einsum("ijr,jck->ickr", windows, first_table, precision=PRECISE)
    return jnp.einsum("pdic,ickr->pdkr", second_table, half, precision=PRECISE)


def cross_of(own_spectrum, later_spectrum, weight):
    own_real = own_spectrum[:, 0]
    own_imag = own_spectrum[:, 1]
    late_real = later_spectrum[:, 0]
    late_imag = later_spectrum[:, 1]
    cross_real = (own_real * late_real + own_imag * late_imag) * weight
    cross_imag = (own_real * late_imag - own_imag * late_real) * weight
    return jnp.stack([cross_real, cross_imag], axis=1)


def back_transform(cross, third_table, fourth_table):
    middle = jnp.einsum("pckr,ckdv->pdvr", cross, third_table, precision=PRECISE)
    return jnp.einsum("pdvr,upd->uvr", middle, fourth_table, precision=PRECISE)


def body(frames, validity, anchors):
    current = frames[0]
    pixel_rows, columns = current.shape
    window = WIN
    stride = window // 2
    window_rows = pixel_rows // stride
    lag_count = window // 2
    total_frames = lax.axis_size("tm")
    position = lax.axis_index("tm")
    first_table, second_table, third_table, fourth_table = tables(window, lag_count)
    own_valid = validity[0].astype(jnp.float32)
    padded_own = jnp.pad(current, ((0, 2 * stride), (0, 2 * stride)))
    windows = cut_windows(padded_own, anchors[0], anchors[1], window_rows, window, columns)
    own_spectrum = spectrum(windows, first_table, second_table)
    results = []
    for distance in DISTANCES:
        partner, partner_valid = shifted_2((own_spectrum, own_valid), "tm", -distance)
        later_index = position + distance
        inside = (later_index < total_frames).astype(jnp.float32)
        scale = 1.0 / (float(total_frames - distance) * float(window) ** 4)
        weight = own_valid * partner_valid * inside * scale
        results.append(
            back_transform(cross_of(own_spectrum, partner, weight), third_table, fourth_table)
        )
    partial_value = jnp.stack(results)
    return lax.psum_scatter(partial_value, "tm", scatter_dimension=3, tiled=True)


GROUP = 16
BF = jnp.bfloat16
F32 = jnp.float32


def halves(table):
    table = table.astype(np.float32)
    high = table.astype(ml_dtypes.bfloat16)
    low = (table - high.astype(np.float32)).astype(ml_dtypes.bfloat16)
    return high, low


@functools.cache
def constant_tables():
    unit = 2.0 * np.pi / 64
    cols = np.arange(160)[:, None]
    wide = np.zeros((160, 384))
    k = np.arange(32)[None, :]
    for b in range(4):
        inside = (cols >= 32 * b) & (cols < 32 * b + 64)
        wide[:, 32 * b : 32 * b + 32] = np.cos(unit * (cols * k % 64)) * inside
        wide[:, 128 + 32 * b : 160 + 32 * b] = -np.sin(unit * (cols * k % 64)) * inside
        wide[:, 256 + b] = ((1 - 2 * (cols % 2)) * inside)[:, 0]
    high, low = halves(wide)
    w1 = np.concatenate([high[:128], high[:128]], axis=0)
    w2 = np.concatenate(
        [low[:128], high[128:], high[128:], low[128:], np.zeros_like(low[128:])], axis=0
    )
    p = np.arange(64)
    angle = unit * (p[:, None] * p[None, :] % 64)
    high, low = halves(np.concatenate([np.cos(angle), np.sin(angle)] * 2, axis=0))
    m = np.concatenate([high, high, low], axis=1)
    u = np.arange(32) - 16
    angle = unit * (u[:, None] * p[None, :] % 64)
    cosine, sine = np.cos(angle), np.sin(angle)
    high, low = halves(
        np.concatenate(
            [np.concatenate([cosine, -sine], axis=1), np.concatenate([sine, cosine], axis=1)],
            axis=0,
        )
    )
    g = np.concatenate([high, high, low], axis=1)
    back = np.zeros((384, 128))
    twice = np.where(np.arange(32) == 0, 1.0, 2.0)[:, None]
    angle = unit * (np.arange(32)[:, None] * u[None, :] % 64)
    for b in range(4):
        span = slice(32 * b, 32 * b + 32)
        back[span, span] = twice * np.cos(angle)
        back[128 + b, span] = 1 - 2 * (u % 2)
        back[256 + 32 * b : 288 + 32 * b, span] = -twice * np.sin(angle)
    high, low = halves(back)
    h = np.concatenate([high, low], axis=1)
    return w1, w2, m, g, h


def column_block(device):
    return lax.rem(device, 8) * 2 + device // 8


def split(value):
    high = value.astype(BF)
    return high, (value - high.astype(F32)).astype(BF)


def dot(left, right):
    return jnp.dot(left, right, preferred_element_type=F32)


def kernel(
    anchor_hbm, x_hbm, v_hbm, w1_hbm, w2_hbm, m_hbm, g_hbm, h_hbm, out_ref,
    anchor_ref, x_ref, v_ref, w1_ref, w2_ref, m_ref, g_ref, h_ref, load_sem, pack, recv, mask_m, expand, sre, sim, cross, lag, plane,
    own, got, send_sem, recv_sem, plane_send, plane_recv,
):
    me = lax.axis_index("tm")
    side = me // 8
    partner = lax.rem(me + 8, GROUP)
    mine = column_block(me)

    barrier = pltpu.get_barrier_semaphore()
    for step in range(1, GROUP):
        peer = lax.rem(me + step, GROUP)
        pl.semaphore_signal(
            barrier, inc=1, device_id={"tm": peer}, device_id_type=pl.DeviceIdType.MESH
        )

    loads = [
        pltpu.make_async_copy(source, target, load_sem.at[index])
        for index, (source, target) in enumerate(
            [
                (anchor_hbm, anchor_ref),
                (x_hbm, x_ref),
                (v_hbm, v_ref),
                (m_hbm, m_ref),
                (w1_hbm, w1_ref),
                (w2_hbm, w2_ref),
                (g_hbm, g_ref),
                (h_hbm, h_ref),
            ]
        )
    ]
    for load in loads:
        load.start()
    for load in loads[:3]:
        load.wait()
    row_start = anchor_ref[0]
    col_start = anchor_ref[1]

    lane = lax.broadcasted_iota(jnp.int32, (64, 128), 1)
    lane16 = lax.broadcasted_iota(jnp.int32, (16, 128), 1)
    keep = lane < 128 - col_start
    amount = lax.rem(128 - col_start, 128)
    valid_row = jnp.broadcast_to(v_ref[...].astype(F32), (8, 128))
    following = jnp.zeros((64, 128), F32)
    halo = jnp.zeros((16, 128), F32)
    for block in reversed(range(GROUP)):
        rolled = pltpu.roll(x_ref[:, 128 * block : 128 * block + 128], amount, 1)
        shifted = jnp.where(keep, rolled, following)
        pack[block, 0:64, :] = shifted
        pack[block, 64:80, :] = halo
        pack[block, 80:88, :] = valid_row
        following = rolled
        halo = shifted[0:16]
        for group in range(1, 4):
            moved = pltpu.roll(shifted[16 * group : 16 * group + 16], 32 * group, 1)
            halo = jnp.where(lane16 >= 32 * group, moved, halo)

    pl.semaphore_wait(barrier, GROUP - 1)

    def transfer(source, target):
        return pltpu.make_async_remote_copy(
            src_ref=pack.at[column_block(target), pl.ds(0, 81)],
            dst_ref=recv.at[source, pl.ds(0, 81)],
            send_sem=send_sem.at[target],
            recv_sem=recv_sem.at[source],
            device_id={"tm": target},
            device_id_type=pl.DeviceIdType.MESH,
        )

    for step in range(8):
        transfer(me, 8 * (1 - side) + lax.rem(me + step, 8)).start()
    for step in range(1, 8):
        transfer(me, 8 * side + lax.rem(me + step, 8)).start()

    for load in loads[3:]:
        load.wait()
    row = lax.rem(lax.broadcasted_iota(jnp.int32, (256, 192), 1), 64)
    below = row_start + 32 * (lax.broadcasted_iota(jnp.int32, (256, 192), 0) // 128)
    mask_m[...] = jnp.where(row >= below, m_ref[...].astype(F32), 0.0).astype(BF)
    region = lax.broadcasted_iota(jnp.int32, (128, 512), 0)
    place = lax.broadcasted_iota(jnp.int32, (128, 512), 1)
    inner = lax.rem(place, 256)
    which = jnp.where(inner < 128, inner // 32, inner - 128)
    wanted = 64 * (place // 256) + 4 * mine + which
    expand[...] = jnp.where((region == wanted) & (which < 4), 1.0, 0.0).astype(BF)

    def operands(t):
        main_high, main_low = split(recv[t, 0:64, :])
        edge = recv[t, 64:80, :]
        edge_high = edge.astype(BF).astype(F32)
        edge_low = edge - edge_high
        tiles = []
        for group in range(4):
            first = pltpu.roll(edge_high, (128 - 32 * group) % 128, 1)
            second = pltpu.roll(edge_low, (160 - 32 * group) % 128, 1)
            third = pltpu.roll(edge_high, (192 - 32 * group) % 128, 1)
            tile = jnp.where(lane16 < 32, first, jnp.where(lane16 < 64, second, third))
            tiles.append(jnp.where(lane16 < 96, tile, 0.0))
        edges = jnp.concatenate(tiles, axis=0).astype(BF)
        return (
            jnp.concatenate([main_high, main_low], axis=1),
            jnp.concatenate([main_high, edges], axis=1),
        )

    def spectra(times):
        pairs = [operands(t) for t in times]
        halved = dot(jnp.concatenate([pair[0] for pair in pairs], axis=0), w1_ref[...])
        halved += dot(jnp.concatenate([pair[1] for pair in pairs], axis=0), w2_ref[...])
        flags = jnp.concatenate([recv[t, 80:81, :] for t in times] * 2, axis=0)
        usable = dot(flags.astype(BF), expand[...])
        for slot, t in enumerate(times):
            half_high, half_low = split(halved[64 * slot : 64 * slot + 64])
            full = dot(mask_m[...], jnp.concatenate([half_high, half_low, half_high], axis=0))
            for a in range(2):
                cos_part = full[128 * a : 128 * a + 64]
                sin_part = full[128 * a + 64 : 128 * a + 128]
                weight = usable[slot : slot + 1, 256 * a : 256 * a + 256]
                main, last = weight[:, 0:128], weight[:, 128:256]
                sre[t, a, :, 0:128] = (cos_part[:, 0:128] + sin_part[:, 128:256]) * main
                sim[t, a, :, 0:128] = (cos_part[:, 128:256] - sin_part[:, 0:128]) * main
                sre[t, a, :, 128:256] = cos_part[:, 256:384] * last
                sim[t, a, :, 128:256] = -sin_part[:, 256:384] * last

    def source_of(step):
        near = step < 8
        return 8 * jnp.where(near, side, 1 - side) + lax.rem(me - step + GROUP, 8)

    recv[me] = pack[mine]
    for step in range(1, 4):
        transfer(source_of(step), me).wait_recv()
    spectra([source_of(step) for step in range(4)])

    def arrive(batch, carry):
        sources = [source_of(4 * batch + step) for step in range(4)]
        for source in sources:
            transfer(source, me).wait_recv()
        spectra(sources)
        return carry

    lax.fori_loop(1, 4, arrive, 0)

    def correlate(a, index, carry):
        start = pl.multiple_of(index * 8, 8)
        line = lax.broadcasted_iota(jnp.int32, (8, 128), 0) + start
        column = lax.rem(lax.broadcasted_iota(jnp.int32, (8, 128), 1), 32)
        for part in range(2):
            lanes = slice(128 * part, 128 * part + 128)
            real = [sre[t, a, pl.ds(start, 8), lanes] for t in range(GROUP)]
            imag = [sim[t, a, pl.ds(start, 8), lanes] for t in range(GROUP)]
            for e, distance in enumerate(DISTANCES):
                total_real = jnp.zeros((8, 128), F32)
                total_imag = jnp.zeros((8, 128), F32)
                for t in range(GROUP - distance):
                    later = t + distance
                    total_real += real[t] * real[later] + imag[t] * imag[later]
                    total_imag += real[t] * imag[later] - imag[t] * real[later]
                scale = 1.0 / (float(GROUP - distance) * float(WIN) ** 4)
                if part == 0:
                    alive = (line > 0) | (column > 0)
                    total_real = jnp.where(alive, total_real, 0.0)
                    total_imag = jnp.where(alive, total_imag, 0.0)
                cross[e, a, pl.ds(start, 8), lanes] = total_real * scale
                cross[e, a, pl.ds(start + 64, 8), lanes] = total_imag * scale
        return carry

    def back(a):
        for e in range(4):
            high, low = split(cross[e, a])
            middle = dot(g_ref[...], jnp.concatenate([high, low, high], axis=0))
            lag[32 * e : 32 * e + 32, 0:256] = middle[0:32]
            lag[32 * e : 32 * e + 32, 256:384] = middle[32:64, 0:128]
        high, low = split(lag[...])
        both = dot(high, h_ref[...])
        return both[:, 0:128] + both[:, 128:256] + dot(low, h_ref[:, 0:128])

    lax.fori_loop(0, 8, functools.partial(correlate, 1 - side), 0)
    plane[...] = back(1 - side)
    give = pltpu.make_async_remote_copy(
        src_ref=plane,
        dst_ref=got,
        send_sem=plane_send,
        recv_sem=plane_recv,
        device_id={"tm": partner},
        device_id_type=pl.DeviceIdType.MESH,
    )
    give.start()
    lax.fori_loop(0, 8, functools.partial(correlate, side), 0)
    own[...] = back(side)

    def place_out(half, planes):
        for b in range(4):
            out_ref[:, 4 * half + b, :] = planes[:, 32 * b : 32 * b + 32]

    for half in range(2):

        @pl.when(side == half)
        def _():
            place_out(half, own[...])

    for step in range(1, GROUP):
        transfer(me, lax.rem(me + step, GROUP)).wait_send()
    give.wait()
    for half in range(2):

        @pl.when(side == 1 - half)
        def _():
            place_out(half, got[...])


def group_body(frames, validity, anchors):
    tables_in = [jnp.asarray(table) for table in constant_tables()]
    vmem = pl.BlockSpec(memory_space=pltpu.VMEM)
    tiles = pl.pallas_call(
        kernel,
        out_shape=jax.ShapeDtypeStruct((128, 8, 32), F32),
        in_specs=[pl.BlockSpec(memory_space=pltpu.HBM)] * 8,
        out_specs=vmem,
        scratch_shapes=[
            pltpu.SMEM((2,), jnp.int32),
            pltpu.VMEM(frames.shape[1:], F32),
            pltpu.VMEM(validity.shape, jnp.int32),
            *[pltpu.VMEM(table.shape, BF) for table in tables_in],
            pltpu.SemaphoreType.DMA((8,)),
            pltpu.VMEM((GROUP, 88, 128), F32),
            pltpu.VMEM((GROUP, 88, 128), F32),
            pltpu.VMEM((256, 192), BF),
            pltpu.VMEM((128, 512), BF),
            pltpu.VMEM((GROUP, 2, 64, 256), F32),
            pltpu.VMEM((GROUP, 2, 64, 256), F32),
            pltpu.VMEM((4, 2, 128, 256), F32),
            pltpu.VMEM((128, 384), F32),
            *[pltpu.VMEM((128, 128), F32)] * 3,
            pltpu.SemaphoreType.DMA((GROUP,)),
            pltpu.SemaphoreType.DMA((GROUP,)),
            pltpu.SemaphoreType.DMA,
            pltpu.SemaphoreType.DMA,
        ],
        compiler_params=pltpu.CompilerParams(
            collective_id=0, has_side_effects=True, vmem_limit_bytes=60 * 1024 * 1024
        ),
    )(anchors, frames[0], validity, *tables_in)
    return tiles.reshape(4, 32, 8, 32).transpose(0, 1, 3, 2)


def solution(mesh):
    placed = (P(("runs", "tm"), None, None), P(("runs", "tm"), None), P("runs"))
    chosen = group_body if mesh.shape["tm"] == GROUP else body
    return jax.shard_map(
        chosen, mesh=mesh, in_specs=placed, out_specs=P("runs", None, None, "tm"), check_vma=False
    )
```
